512 devices in a mesh: replica: 32 (over y, x, core), tensor: 16 (over z).
Axes of the slice: x: 4, y: 4, z: 16, core: 2. Of those that a mesh axis runs over, the one named last changes fastest.
Arguments:
- tokens: bfloat16 [16384, 8192], P('replica', 'tensor'), may hold values from -6 to 6
- cotangent: bfloat16 [16384, 512], P(('replica', 'tensor')), may hold values from -6 to 6
- drift: bfloat16 [32, 512, 8192], P('replica', None, 'tensor'), may hold values from -8 to 8
- error: bfloat16 [32, 512, 8192], P('replica', None, 'tensor'), may hold values from -3 to 3
- weight: float32 [512, 8192], P('replica', 'tensor'), may hold values from -6 to 6
- momentum: float32 [512, 8192], P('replica', 'tensor'), may hold values from -3 to 3
- factor: float32 [32, 8192], P(None, 'tensor'), may hold values from -6 to 6
- gain: float32 [128], replicated, may hold values from 0.1 to 1.9
Outputs:
- new_weight: float32 [512, 8192], P('replica', 'tensor')
- new_momentum: float32 [512, 8192], P('replica', 'tensor')
- new_error: bfloat16 [32, 512, 8192], P('replica', None, 'tensor')
- new_factor: float32 [32, 8192], P(None, 'tensor')
- weight_grad: bfloat16 [32, 512, 8192], P('replica', None, 'tensor')
The draws below stay inside these ranges and needn't reach their ends.
All inputs are finite; a program needn't handle non-finite values.
Results may differ from the reference program's by a relative error of at most 0.015.
Values may be sent and summed in bfloat16 or wider, within the bound.
A program may use at most 64 MiB of HBM per device.

```python
import math
import jax
import jax.numpy as jnp
from jax import lax

D = 8192
HD = 128
KEYS = 512
R = 32
TOK = 512
REPLICAS = 32
TOKENS = 16384


def draw_drift(key, part):
    key = jax.random.fold_in(key, 11)
    shared_key, own_key = jax.random.split(key)
    shared = jax.random.normal(shared_key, (1, KEYS, D), jnp.float32)
    own = jax.random.normal(own_key, (REPLICAS, KEYS, D), jnp.float32)
    return jnp.clip(shared + own, -8.0, 8.0).astype(jnp.bfloat16)


def shard_levels(stream_key, dims, pieces, least, top_value):
    loudness = 1.0
    for axis_at, parts in pieces:
        heights = jax.random.uniform(jax.random.fold_in(jax.random.fold_in(stream_key, 6), axis_at), (parts,), jnp.float32, least / len(pieces), top_value / len(pieces))
        loudness = loudness * jnp.repeat(jnp.exp(heights), dims[axis_at] // parts).reshape((-1,) + (1,) * (len(dims) - 1 - axis_at))
    return loudness


def centred(rng, extent, scale, reach, cuts=(), kind=jnp.bfloat16):
    array = jax.random.normal(rng, extent, jnp.float32) * scale
    if len(cuts) > 0:
        array = shard_levels(rng, extent, cuts, -0.22, 0.18) * array
    return jnp.clip(array, min=-reach, max=reach).astype(kind)


def setup_inputs(seed: int = 0) -> dict:
    key_list = jax.random.split(jax.random.key(seed), 9)
    return {
        "tokens": centred(key_list[0], (TOKENS, D), 1.0, 6.0, ((0, 32), (1, 16))),
        "cotangent": centred(key_list[1], (TOKENS, KEYS), 1.0, 6.0, ((0, 512),)),
        "drift": draw_drift(jax.random.fold_in(key_list[8], 71), 0),
        "error": centred(key_list[3], (REPLICAS, KEYS, D), 0.5, 3.0, ((0, 32), (2, 16))),
        "weight": centred(key_list[4], (KEYS, D), 1.0, 6.0, ((0, 32), (1, 16)), jnp.float32),
        "momentum": centred(key_list[5], (KEYS, D), 0.5, 3.0, ((0, 32), (1, 16)), jnp.float32),
        "factor": centred(key_list[6], (R, D), 1.0, 6.0, ((1, 16),), jnp.float32),
        "gain": jnp.clip(1.0 + 0.18 * jax.random.normal(key_list[7], (HD,), jnp.float32), 0.1, 1.9),
    }


highest = lax.Precision.HIGHEST
outer_rate = 0.7
outer_beta = 0.9

def contract(left, right, left_dim, right_dim):
    return lax.dot_general(left.astype(jnp.float32), right.astype(jnp.float32), (((left_dim,), (right_dim,)), ((), ())), precision=highest, preferred_element_type=jnp.float32)

def orthonormal(left):
    gram = contract(left, left, 1, 1)
    shift = 0.001 * jnp.trace(gram) / left.shape[0] + 1e-06
    lower = jnp.linalg.cholesky(gram + shift * jnp.eye(left.shape[0], dtype=jnp.float32))
    return jax.scipy.linalg.solve_triangular(lower, left, lower=True)

def key_grad(keys, cotangent, gain):
    count = keys.shape[0]
    width = gain.shape[0]
    shaped = keys.reshape(count, -1, width)
    weighted = gain * cotangent.astype(jnp.float32).reshape(count, -1, width)
    inverse = lax.rsqrt(lax.optimization_barrier(jnp.mean(shaped * shaped, axis=2, keepdims=True)) + 1e-06)
    inner = lax.optimization_barrier(jnp.sum(weighted * shaped, axis=2, keepdims=True))
    result = weighted * inverse - shaped * inverse * inverse * inverse * inner / width
    return result.reshape(count, -1).astype(jnp.bfloat16)

def reference(tokens, cotangent, drift, error, weight, momentum, factor, gain):
    replicas = drift.shape[0]

    def add_left(total, pair):
        merged = pair[0].astype(jnp.float32) + pair[1].astype(jnp.float32)
        return (total + contract(factor, merged, 1, 1), None)
    left, _ = lax.scan(add_left, jnp.zeros((R, KEYS), jnp.float32), (drift, error))
    left = left / replicas
    ortho = orthonormal(left)

    def add_right(total, pair):
        merged = pair[0].astype(jnp.float32) + pair[1].astype(jnp.float32)
        return (total + contract(ortho, merged, 1, 0), None)
    right, _ = lax.scan(add_right, jnp.zeros((R, D), jnp.float32), (drift, error))
    new_factor = right / replicas
    approx = contract(ortho, new_factor, 0, 0)

    def residue(pair):
        merged = pair[0].astype(jnp.float32) + pair[1].astype(jnp.float32)
        return (merged - approx).astype(jnp.bfloat16)
    new_error = lax.map(residue, (drift, error))
    new_momentum = outer_beta * momentum + approx
    new_weight = weight - outer_rate * (approx + outer_beta * new_momentum)
    rounded = new_weight.astype(jnp.bfloat16)
    scale = 1.0 / math.sqrt(D)

    def worker_grad(pair):
        inputs, upstream = pair
        keys = lax.dot_general(inputs.astype(jnp.float32), rounded.astype(jnp.float32), (((1,), (1,)), ((), ())), preferred_element_type=jnp.float32) * scale
        grads = key_grad(keys, upstream, gain)
        summed = lax.dot_general(grads.astype(jnp.float32), inputs.astype(jnp.float32), (((0,), (0,)), ((), ())), preferred_element_type=jnp.float32)
        return (summed * scale).astype(jnp.bfloat16)
    weight_grad = lax.map(worker_grad, (tokens.reshape(replicas, TOK, D), cotangent.reshape(replicas, TOK, KEYS)))
    return (new_weight, new_momentum, new_error, new_factor, weight_grad)
```

```python
import functools
import math

import jax
import jax.numpy as jnp
from jax import lax
from jax.experimental import pallas as pl
from jax.experimental.pallas import tpu as pltpu
from jax.sharding import PartitionSpec as P

MESH = pl.DeviceIdType.MESH
highest = lax.Precision.HIGHEST
f32 = jnp.float32
bf16 = jnp.bfloat16
outer_rate = 0.7
outer_beta = 0.9
LANES = 128
GROUP = 8


def dot(left, right, left_dim, right_dim, precision=None):
    return lax.dot_general(
        left,
        right,
        (((left_dim,), (right_dim,)), ((), ())),
        precision=precision,
        preferred_element_type=f32,
    )


def split_dot(left, right, left_dim, right_dim):
    high = left.astype(bf16)
    low = (left - high.astype(f32)).astype(bf16)
    return dot(high, right, left_dim, right_dim) + dot(low, right, left_dim, right_dim)


def send(src, dst, send_sem, recv_sem, device):
    pltpu.make_async_remote_copy(
        src_ref=src,
        dst_ref=dst,
        send_sem=send_sem,
        recv_sem=recv_sem,
        device_id=device,
        device_id_type=MESH,
    ).start()


def drain(ref, sem):
    pltpu.make_async_copy(ref, ref, sem).wait()


def each_other(count, me, act):
    def step(i, carry):
        half = (i + 1) // 2
        offset = count // 2 + half * (2 * (i % 2) - 1)
        act(lax.rem(me + offset, count))
        return carry

    lax.fori_loop(0, count - 1, step, 0)


def pack(rows, rank):
    groups = rows.shape[1] // GROUP
    total = rows[:, 0:GROUP]
    for g in range(1, groups):
        total = total + pltpu.roll(rows[:, g * GROUP : (g + 1) * GROUP], g * rank, 2)
    return total


def unpack(packed, groups, rank):
    lane = lax.broadcasted_iota(jnp.int32, packed.shape, 2)
    parts = []
    for g in range(groups):
        turned = packed if g == 0 else pltpu.roll(packed, LANES - g * rank, 2)
        parts.append(jnp.where(lane < rank, turned, 0.0))
    return jnp.concatenate(parts, axis=1)


def inverse_factor(gram, rank):
    row = lax.broadcasted_iota(jnp.int32, (rank, LANES), 0)
    lane = lax.broadcasted_iota(jnp.int32, (rank, LANES), 1)
    diagonal = row == lane
    trace = jnp.sum(
        jnp.sum(jnp.where(diagonal, gram, 0.0), axis=1, keepdims=True), axis=0, keepdims=True
    )
    shift = 0.001 * trace / rank + 1e-06
    a = jnp.where(lane < rank, gram, 0.0) + jnp.where(diagonal, shift, 0.0)
    a = a + jnp.where(lane == row + rank, 1.0, 0.0)
    down = lax.broadcasted_iota(jnp.int32, (rank, 1), 0)
    for k in range(rank - 1):
        pivot_row = a[k : k + 1, :]
        share = pivot_row * (1.0 / pivot_row[:, k : k + 1])
        column = jnp.where(down > k, a[:, k : k + 1], 0.0)
        a = a - column * share
    pivots = jnp.sum(jnp.where(diagonal, a, 0.0), axis=1, keepdims=True)
    a = a * (1.0 / jnp.sqrt(pivots))
    return jnp.where(lane < rank, pltpu.roll(a, LANES - rank, 1), 0.0)


def key_grad(keys, cotangent, gain):
    width = gain.shape[1]
    parts = []
    for head in range(keys.shape[1] // width):
        at = slice(head * width, (head + 1) * width)
        shaped = keys[:, at]
        weighted = gain * cotangent[:, at]
        inverse = lax.rsqrt(jnp.mean(shaped * shaped, axis=1, keepdims=True) + 1e-06)
        inner = jnp.sum(weighted * shaped, axis=1, keepdims=True)
        parts.append(
            weighted * inverse - shaped * (inverse * inverse * inverse * inner / width)
        )
    return jnp.concatenate(parts, axis=1)


def kernel(
    nr, nz, scale,
    tokens, cotangent, drift, error, weight, momentum, factor, gain,
    new_weight, new_momentum, new_error, new_factor, weight_grad,
    mb, pb, ps, mr, ub, mg, lz, la, lt, kb, kr, pp, pr, ga, ss, rs,
):
    r = lax.axis_index("replica")
    z = lax.axis_index("tensor")
    chips = nr // 2
    chip, core = r // 2, lax.rem(r, 2)
    other = 1 - core
    partner = {"replica": chip * 2 + other}
    rank, width = factor.shape
    keys = drift.shape[0]
    rows = weight.shape[0]
    mine = tokens.shape[0] // nz

    def across(chip_at):
        return {"replica": chip_at * 2 + core}

    barrier = pltpu.get_barrier_semaphore()

    def greet_replica(peer):
        pl.semaphore_signal(barrier, inc=1, device_id={"replica": peer}, device_id_type=MESH)

    def greet_tensor(peer):
        pl.semaphore_signal(barrier, inc=1, device_id={"tensor": peer}, device_id_type=MESH)

    each_other(nz, z, greet_tensor)
    each_other(nr, r, greet_replica)

    mb[...] = (drift[...].astype(f32) + error[...].astype(f32)).astype(bf16).reshape(mb.shape)
    base = weight[...] - (outer_rate * outer_beta * outer_beta) * momentum[...]
    ub[chip, core] = base.astype(bf16)
    pl.semaphore_wait(barrier, nr + nz - 2)

    send(mb.at[:, other], pb, ss.at[0], rs.at[0], partner)
    each_other(
        chips, chip,
        lambda p: send(ub.at[chip, core], ub.at[chip, core], ss.at[1], rs.at[1], across(p)),
    )
    drain(pb, rs.at[0])
    ps[...] = (mb[:, pl.ds(core, 1)][:, 0].astype(f32) + pb[...].astype(f32)).astype(bf16)
    each_other(
        chips, chip,
        lambda p: send(ps.at[p], mr.at[chip], ss.at[2], rs.at[2], across(p)),
    )
    mr[chip] = ps[chip]

    drain(ps.at[pl.ds(0, chips - 1)], rs.at[1])
    send(ub.at[:, core], ub.at[:, core], ss.at[3], rs.at[3], partner)

    drain(ps.at[pl.ds(0, chips - 1)], rs.at[2])
    mean = jnp.sum(mr[...].astype(f32), axis=0) * (1.0 / nr)
    padded = jnp.concatenate([factor[...], jnp.zeros((LANES - rank, width), f32)], axis=0)
    term = dot(mean, padded, 1, 1, highest)
    lz[z] = pack(term[None], rank)[0]
    each_other(
        nz, z,
        lambda p: send(lz.at[z], lz.at[z], ss.at[4], rs.at[4], {"tensor": p}),
    )
    mg[chip, core] = mean.astype(bf16)
    each_other(
        chips, chip,
        lambda p: send(mg.at[chip, core], mg.at[chip, core], ss.at[5], rs.at[5], across(p)),
    )

    drain(pb, rs.at[3])
    partial = dot(tokens[...], ub[...].reshape(keys, width), 1, 1) * scale
    kb[...] = partial.astype(bf16).reshape(kb.shape)
    each_other(
        nz, z,
        lambda p: send(kb.at[p], kr.at[z], ss.at[6], rs.at[6], {"tensor": p}),
    )
    kr[z] = kb[z]

    drain(ps.at[pl.ds(0, chips - 1)], rs.at[5])
    send(mg.at[:, core], mg.at[:, core], ss.at[7], rs.at[7], partner)

    drain(lz.at[pl.ds(0, nz - 1)], rs.at[4])
    la[r] = jnp.sum(lz[...], axis=0)
    each_other(
        nr, r,
        lambda p: send(la.at[r], la.at[r], ss.at[8], rs.at[8], {"replica": p}),
    )
    drain(pb, rs.at[7])
    drain(la.at[pl.ds(0, nr - 1)], rs.at[8])
    left = unpack(la[...], rows // GROUP, rank)
    lt[...] = left.reshape(lt.shape)
    left = left.reshape(keys, LANES)
    gram = dot(left, left, 0, 0, highest)[0:rank]
    inverse = inverse_factor(gram, rank)
    ortho = dot(inverse, left, 1, 1, highest)
    right = split_dot(ortho, mg[...].reshape(keys, width), 1, 0)
    new_factor[...] = right
    zeros = jnp.zeros((LANES - rank, width), f32)
    right_padded = jnp.concatenate([right, zeros], axis=0)
    product = dot(tokens[...], right_padded.astype(bf16), 1, 1)
    pp[...] = pack(product.reshape(nz, mine, LANES), rank)
    each_other(
        nz, z,
        lambda p: send(pp.at[p], pr.at[z], ss.at[9], rs.at[9], {"tensor": p}),
    )
    pr[z] = pp[z]

    inverse_padded = jnp.concatenate([inverse, jnp.zeros((LANES - rank, LANES), f32)], axis=0)
    own_ortho = dot(lt[r], inverse_padded, 1, 1, highest)
    own_approx = dot(own_ortho, right_padded, 1, 0, highest)
    next_momentum = outer_beta * momentum[...] + own_approx
    new_momentum[...] = next_momentum
    new_weight[...] = weight[...] - outer_rate * (own_approx + outer_beta * next_momentum)
    ortho_rows = dot(left, inverse_padded, 1, 1).astype(bf16)
    approx = dot(ortho_rows, right_padded.astype(bf16), 1, 0)
    merged = drift[...].astype(f32) + error[...].astype(f32)
    new_error[...] = (merged - approx).astype(bf16)

    drain(kb.at[pl.ds(0, nz - 1)], rs.at[6])
    base_keys = jnp.sum(kr[...].astype(f32), axis=0)
    drain(pp.at[pl.ds(0, nz - 1)], rs.at[9])
    summed = unpack(jnp.sum(pr[...], axis=0)[None], mine // GROUP, rank)[0]
    ortho_padded = jnp.concatenate([ortho, jnp.zeros((LANES - rank, keys), f32)], axis=0)
    turn = dot(summed, ortho_padded, 1, 0, highest)
    own_keys = base_keys - (outer_rate * (1.0 + outer_beta) * scale) * turn
    ga[z] = key_grad(own_keys, cotangent[...].astype(f32), gain[...]).astype(bf16)
    each_other(
        nz, z,
        lambda p: send(ga.at[z], ga.at[z], ss.at[10], rs.at[10], {"tensor": p}),
    )
    drain(ga.at[pl.ds(0, nz - 1)], rs.at[10])
    grads = ga[...].reshape(tokens.shape[0], keys)
    weight_grad[...] = (dot(grads, tokens[...], 0, 0) * scale).astype(bf16)

    drain(pb, ss.at[0])
    drain(ps.at[pl.ds(0, chips - 1)], ss.at[1])
    drain(ps.at[pl.ds(0, chips - 1)], ss.at[2])
    drain(pb, ss.at[3])
    drain(lz.at[pl.ds(0, nz - 1)], ss.at[4])
    drain(ps.at[pl.ds(0, chips - 1)], ss.at[5])
    drain(kb.at[pl.ds(0, nz - 1)], ss.at[6])
    drain(pb, ss.at[7])
    drain(la.at[pl.ds(0, nr - 1)], ss.at[8])
    drain(pp.at[pl.ds(0, nz - 1)], ss.at[9])
    drain(ga.at[pl.ds(0, nz - 1)], ss.at[10])


def solution(mesh):
    nr, nz = mesh.shape["replica"], mesh.shape["tensor"]
    chips = nr // 2

    def body(tokens, cotangent, drift, error, weight, momentum, factor, gain):
        count, width = tokens.shape
        keys = drift.shape[1]
        rows = weight.shape[0]
        mine = count // nz
        scale = 1.0 / math.sqrt(width * nz)
        shapes = (
            jax.ShapeDtypeStruct(weight.shape, f32),
            jax.ShapeDtypeStruct(weight.shape, f32),
            jax.ShapeDtypeStruct((keys, width), bf16),
            jax.ShapeDtypeStruct(factor.shape, f32),
            jax.ShapeDtypeStruct((keys, width), bf16),
        )
        in_vmem = pl.BlockSpec(memory_space=pltpu.VMEM)
        out = pl.pallas_call(
            functools.partial(kernel, nr, nz, scale),
            out_shape=shapes,
            in_specs=[in_vmem] * 8,
            out_specs=(in_vmem,) * 5,
            scratch_shapes=[
                pltpu.VMEM((chips, 2, rows, width), bf16),
                pltpu.VMEM((chips, rows, width), bf16),
                pltpu.VMEM((chips, rows, width), bf16),
                pltpu.VMEM((chips, rows, width), bf16),
                pltpu.VMEM((chips, 2, rows, width), bf16),
                pltpu.VMEM((chips, 2, rows, width), bf16),
                pltpu.VMEM((nz, GROUP, LANES), f32),
                pltpu.VMEM((nr, GROUP, LANES), f32),
                pltpu.VMEM((nr, rows, LANES), f32),
                pltpu.VMEM((nz, mine, keys), bf16),
                pltpu.VMEM((nz, mine, keys), bf16),
                pltpu.VMEM((nz, GROUP, LANES), f32),
                pltpu.VMEM((nz, GROUP, LANES), f32),
                pltpu.VMEM((nz, mine, keys), bf16),
                pltpu.SemaphoreType.DMA((11,)),
                pltpu.SemaphoreType.DMA((11,)),
            ],
            compiler_params=pltpu.CompilerParams(
                collective_id=0, has_side_effects=True, vmem_limit_bytes=40 * 1024 * 1024
            ),
            name="outer_inner_step",
        )(
            tokens, cotangent, drift[0], error[0], weight, momentum, factor, gain.reshape(1, -1)
        )
        return (out[0], out[1], out[2][None], out[3], out[4][None])

    placed = (
        P("replica", "tensor"),
        P(("replica", "tensor"), None),
        P("replica", None, "tensor"),
        P("replica", None, "tensor"),
        P("replica", "tensor"),
        P("replica", "tensor"),
        P(None, "tensor"),
        P(),
    )
    return jax.shard_map(
        body,
        mesh=mesh,
        in_specs=placed,
        out_specs=(
            P("replica", "tensor"),
            P("replica", "tensor"),
            P("replica", None, "tensor"),
            P(None, "tensor"),
            P("replica", None, "tensor"),
        ),
        check_vma=False,
    )
```

```python
import functools
import math

import jax
import jax.numpy as jnp
from jax import lax
from jax.experimental import pallas as pl
from jax.experimental.pallas import tpu as pltpu
from jax.sharding import PartitionSpec as P

MESH = pl.DeviceIdType.MESH
highest = lax.Precision.HIGHEST
f32 = jnp.float32
bf16 = jnp.bfloat16
outer_rate = 0.7
outer_beta = 0.9
LANES = 128
GROUP = 8
GRANT = 60 * 1024 * 1024


def dot(left, right, left_dim, right_dim, precision=None):
    return lax.dot_general(
        left,
        right,
        (((left_dim,), (right_dim,)), ((), ())),
        precision=precision,
        preferred_element_type=f32,
    )


def split_dot(left, right, left_dim, right_dim):
    high = left.astype(bf16)
    low = (left - high.astype(f32)).astype(bf16)
    return dot(high, right, left_dim, right_dim) + dot(low, right, left_dim, right_dim)


def send(src, dst, send_sem, recv_sem, device):
    pltpu.make_async_remote_copy(
        src_ref=src,
        dst_ref=dst,
        send_sem=send_sem,
        recv_sem=recv_sem,
        device_id=device,
        device_id_type=MESH,
    ).start()


def drain(ref, sem):
    pltpu.make_async_copy(ref, ref, sem).wait()


def each_other(count, me, act):
    def step(i, carry):
        half = (i + 1) // 2
        offset = count // 2 + half * (2 * (i % 2) - 1)
        act(lax.rem(me + offset, count))
        return carry

    lax.fori_loop(0, count - 1, step, 0)


def pack(rows, rank):
    groups = rows.shape[1] // GROUP
    total = rows[:, 0:GROUP]
    for g in range(1, groups):
        total = total + pltpu.roll(rows[:, g * GROUP : (g + 1) * GROUP], g * rank, 2)
    return total


def unpack(packed, groups, rank):
    lane = lax.broadcasted_iota(jnp.int32, packed.shape, 2)
    parts = []
    for g in range(groups):
        turned = packed if g == 0 else pltpu.roll(packed, LANES - g * rank, 2)
        parts.append(jnp.where(lane < rank, turned, 0.0))
    return jnp.concatenate(parts, axis=1)


def inverse_factor(gram, rank):
    row = lax.broadcasted_iota(jnp.int32, (rank, LANES), 0)
    lane = lax.broadcasted_iota(jnp.int32, (rank, LANES), 1)
    diagonal = row == lane
    trace = jnp.sum(
        jnp.sum(jnp.where(diagonal, gram, 0.0), axis=1, keepdims=True), axis=0, keepdims=True
    )
    shift = 0.001 * trace / rank + 1e-06
    a = jnp.where(lane < rank, gram, 0.0) + jnp.where(diagonal, shift, 0.0)
    a = a + jnp.where(lane == row + rank, 1.0, 0.0)
    down = lax.broadcasted_iota(jnp.int32, (rank, 1), 0)
    for k in range(rank - 1):
        pivot_row = a[k : k + 1, :]
        share = pivot_row * (1.0 / pivot_row[:, k : k + 1])
        column = jnp.where(down > k, a[:, k : k + 1], 0.0)
        a = a - column * share
    pivots = jnp.sum(jnp.where(diagonal, a, 0.0), axis=1, keepdims=True)
    a = a * (1.0 / jnp.sqrt(pivots))
    return jnp.where(lane < rank, pltpu.roll(a, LANES - rank, 1), 0.0)


def key_grad(keys, cotangent, gain):
    width = gain.shape[1]
    parts = []
    for head in range(keys.shape[1] // width):
        at = slice(head * width, (head + 1) * width)
        shaped = keys[:, at]
        weighted = gain * cotangent[:, at]
        inverse = lax.rsqrt(jnp.mean(shaped * shaped, axis=1, keepdims=True) + 1e-06)
        inner = jnp.sum(weighted * shaped, axis=1, keepdims=True)
        parts.append(
            weighted * inverse - shaped * (inverse * inverse * inverse * inner / width)
        )
    return jnp.concatenate(parts, axis=1)


def gather_ring(count, me, ga, ss, rs, at):
    half = ga.shape[1] // 2

    def peer(offset):
        return {"tensor": lax.rem(me + offset + count, count)}

    def block(offset):
        return ga.at[lax.rem(me + offset + count, count)]

    near = at + 2
    send(block(0), block(0), ss.at[at], rs.at[at], peer(5))
    send(block(0), block(0), ss.at[at + 1], rs.at[at + 1], peer(-5))
    for offset in (2, -2, 1, -1):
        send(block(0), block(0), ss.at[near], rs.at[near], peer(offset))
    drain(block(0), rs.at[at])
    low = block(-5).at[pl.ds(0, half)]
    send(low, low, ss.at[near], rs.at[near], peer(3))
    for offset in (2, -2, 1, -1):
        send(block(-5), block(-5), ss.at[near], rs.at[near], peer(offset))
    drain(block(0), rs.at[at + 1])
    high = block(5).at[pl.ds(half, half)]
    send(high, high, ss.at[near], rs.at[near], peer(-3))
    for offset in (2, -2, 1, -1):
        send(block(5), block(5), ss.at[near], rs.at[near], peer(offset))
    drain(ga.at[pl.ds(0, 13)], rs.at[near])
    drain(block(0), ss.at[at])
    drain(block(0), ss.at[at + 1])
    drain(ga.at[pl.ds(0, 13)], ss.at[near])


def scatter_near(count, me, kb, kn, kh, ss, rs, at):
    half = kb.shape[1] // 2

    def index(offset):
        return lax.rem(me + offset + 2 * count, count)

    for far, offset in ((5, 3), (-5, -3)):
        side = 0 if far > 0 else 1
        send(
            kb.at[index(offset + far), pl.ds(side * half, half)], kh.at[side],
            ss.at[at], rs.at[at], {"tensor": index(offset)},
        )
    for i, far in enumerate((5, -5, 0)):
        for j, offset in enumerate((2, -2, 1, -1)):
            send(
                kb.at[index(offset + far)], kn.at[j, i],
                ss.at[at], rs.at[at], {"tensor": index(offset)},
            )


def scatter_far(count, me, kb, kn, kh, ks, kr, ss, rs, at):
    half = kb.shape[1] // 2

    def index(offset):
        return lax.rem(me + offset + 2 * count, count)

    drain(kb.at[pl.ds(0, 13)], rs.at[at])
    for i, far in enumerate((5, -5)):
        total = kb[index(far)].astype(f32)
        for j in range(4):
            total = total + kn[j, i].astype(f32)
        eighth = kh[i].astype(f32)
        blank = jnp.zeros_like(eighth)
        total = total + jnp.concatenate([eighth, blank] if i == 0 else [blank, eighth], axis=0)
        ks[i] = total.astype(bf16)
        send(ks.at[i], kr.at[i], ss.at[at + 1], rs.at[at + 1], {"tensor": index(far)})
    total = kb[me].astype(f32)
    for j in range(4):
        total = total + kn[j, 2].astype(f32)
    return total


def finish(
    scale, nw_at, nm_at, ne_at, nf_at, tokens_at, grads_at,
    nw_out, nm_out, ne_out, nf_out, wg_out,
    nw, nm, ne, nf, tokens, grads, held, in_sems, out_sems,
):
    pairs = (
        (grads_at, grads), (tokens_at, tokens),
        (ne_at, ne), (nf_at, nf), (nw_at, nw), (nm_at, nm),
    )
    ins = [pltpu.make_async_copy(src, dst, in_sems.at[i]) for i, (src, dst) in enumerate(pairs)]
    for copy in ins:
        copy.start()
    outs = []

    def leave(src, dst):
        outs.append(pltpu.make_async_copy(src, dst, out_sems.at[len(outs)]))
        outs[-1].start()

    ins[0].wait()
    ins[1].wait()
    half = held.shape[1]
    for i in range(2):
        left = grads[:, i * half : (i + 1) * half]
        held[i] = (dot(left, tokens[...], 0, 0) * scale).astype(bf16)
        leave(held.at[i], wg_out.at[pl.ds(i * half, half)])
        if i == 0:
            results = ((ne, ne_out), (nf, nf_out), (nw, nw_out), (nm, nm_out))
            for load, (src, dst) in zip(ins[2:], results):
                load.wait()
                leave(src, dst)
    for copy in outs:
        copy.wait()


def kernel(
    nr, nz, scale,
    tokens_at, cotangent_at, drift_at, error_at, weight_at, momentum_at, factor_at, gain_at,
    new_weight_at, new_momentum_at, new_error_at, new_factor_at, grads_at,
    new_weight, new_momentum, new_error, new_factor, ga,
    tokens, cotangent, drift, error, weight, momentum, factor, gain,
    mb, pb, ps, mr, ub, mg, lz, la, lt, kb, kn, kh, ks, kr, pp, pr, ss, rs, ls,
):
    r = lax.axis_index("replica")
    z = lax.axis_index("tensor")
    chips = nr // 2
    chip, core = r // 2, lax.rem(r, 2)
    other = 1 - core
    partner = {"replica": chip * 2 + other}
    rank, width = factor.shape
    keys = drift.shape[0]
    rows = weight.shape[0]
    mine = tokens.shape[0] // nz

    def across(chip_at):
        return {"replica": chip_at * 2 + core}

    loads = [
        pltpu.make_async_copy(src, dst, ls.at[i])
        for i, (src, dst) in enumerate(
            (
                (drift_at, drift),
                (error_at, error),
                (weight_at, weight),
                (momentum_at, momentum),
                (factor_at, factor),
                (tokens_at, tokens),
                (cotangent_at, cotangent),
                (gain_at, gain),
            )
        )
    ]
    for load in loads[:4]:
        load.start()
    barrier = pltpu.get_barrier_semaphore()

    def greet_replica(peer):
        pl.semaphore_signal(barrier, inc=1, device_id={"replica": peer}, device_id_type=MESH)

    def greet_tensor(peer):
        pl.semaphore_signal(barrier, inc=1, device_id={"tensor": peer}, device_id_type=MESH)

    each_other(nz, z, greet_tensor)
    each_other(nr, r, greet_replica)
    for load in loads[4:]:
        load.start()
    for load in loads[:4]:
        load.wait()

    mb[...] = (drift[...].astype(f32) + error[...].astype(f32)).astype(bf16).reshape(mb.shape)
    base = weight[...] - (outer_rate * outer_beta * outer_beta) * momentum[...]
    ub[chip, core] = base.astype(bf16)
    for load in loads[4:]:
        load.wait()
    pl.semaphore_wait(barrier, nr + nz - 2)

    send(mb.at[:, other], pb, ss.at[0], rs.at[0], partner)
    drain(pb, rs.at[0])
    ps[...] = (mb[:, pl.ds(core, 1)][:, 0].astype(f32) + pb[...].astype(f32)).astype(bf16)
    each_other(
        chips, chip,
        lambda p: send(ps.at[p], mr.at[chip], ss.at[2], rs.at[2], across(p)),
    )
    each_other(
        chips, chip,
        lambda p: send(ub.at[chip, core], ub.at[chip, core], ss.at[1], rs.at[1], across(p)),
    )
    mr[chip] = ps[chip]

    drain(ps.at[pl.ds(0, chips - 1)], rs.at[1])
    send(ub.at[:, core], ub.at[:, core], ss.at[3], rs.at[3], partner)

    drain(ps.at[pl.ds(0, chips - 1)], rs.at[2])
    mean = jnp.sum(mr[...].astype(f32), axis=0) * (1.0 / nr)
    padded = jnp.concatenate([factor[...], jnp.zeros((LANES - rank, width), f32)], axis=0)
    term = dot(mean, padded, 1, 1, highest)
    lz[z] = pack(term[None], rank)[0]
    each_other(
        nz, z,
        lambda p: send(lz.at[z], lz.at[z], ss.at[4], rs.at[4], {"tensor": p}),
    )
    mg[chip, core] = mean.astype(bf16)
    each_other(
        chips, chip,
        lambda p: send(mg.at[chip, core], mg.at[chip, core], ss.at[5], rs.at[5], across(p)),
    )

    drain(pb, rs.at[3])
    partial = dot(tokens[...], ub[...].reshape(keys, width), 1, 1) * scale
    kb[...] = partial.astype(bf16).reshape(kb.shape)
    scatter_near(nz, z, kb, kn, kh, ss, rs, 13)

    drain(ps.at[pl.ds(0, chips - 1)], rs.at[5])
    send(mg.at[:, core], mg.at[:, core], ss.at[7], rs.at[7], partner)

    drain(lz.at[pl.ds(0, nz - 1)], rs.at[4])
    la[r] = jnp.sum(lz[...], axis=0)
    each_other(
        nr, r,
        lambda p: send(la.at[r], la.at[r], ss.at[8], rs.at[8], {"replica": p}),
    )
    near_keys = scatter_far(nz, z, kb, kn, kh, ks, kr, ss, rs, 13)
    drain(pb, rs.at[7])
    drain(la.at[pl.ds(0, nr - 1)], rs.at[8])
    left = unpack(la[...], rows // GROUP, rank)
    lt[...] = left.reshape(lt.shape)
    left = left.reshape(keys, LANES)
    gram = dot(left, left, 0, 0, highest)[0:rank]
    inverse = inverse_factor(gram, rank)
    ortho = dot(inverse, left, 1, 1, highest)
    right = split_dot(ortho, mg[...].reshape(keys, width), 1, 0)
    new_factor[...] = right
    zeros = jnp.zeros((LANES - rank, width), f32)
    right_padded = jnp.concatenate([right, zeros], axis=0)
    product = dot(tokens[...], right_padded.astype(bf16), 1, 1)
    pp[...] = pack(product.reshape(nz, mine, LANES), rank)
    each_other(
        nz, z,
        lambda p: send(pp.at[p], pr.at[z], ss.at[9], rs.at[9], {"tensor": p}),
    )
    pr[z] = pp[z]

    inverse_padded = jnp.concatenate([inverse, jnp.zeros((LANES - rank, LANES), f32)], axis=0)
    own_ortho = dot(lt[r], inverse_padded, 1, 1, highest)
    own_approx = dot(own_ortho, right_padded, 1, 0, highest)
    next_momentum = outer_beta * momentum[...] + own_approx
    new_momentum[...] = next_momentum
    new_weight[...] = weight[...] - outer_rate * (own_approx + outer_beta * next_momentum)
    ortho_rows = dot(left, inverse_padded, 1, 1).astype(bf16)
    approx = dot(ortho_rows, right_padded.astype(bf16), 1, 0)
    merged = drift[...].astype(f32) + error[...].astype(f32)
    new_error[...] = (merged - approx).astype(bf16)

    stores = [
        pltpu.make_async_copy(src, dst, ls.at[i])
        for i, (src, dst) in enumerate(
            (
                (new_error, new_error_at),
                (new_factor, new_factor_at),
                (new_weight, new_weight_at),
                (new_momentum, new_momentum_at),
            )
        )
    ]
    for store in stores:
        store.start()

    drain(kr, rs.at[14])
    base_keys = near_keys + kr[0].astype(f32) + kr[1].astype(f32)
    drain(pp.at[pl.ds(0, nz - 1)], rs.at[9])
    summed = unpack(jnp.sum(pr[...], axis=0)[None], mine // GROUP, rank)[0]
    ortho_padded = jnp.concatenate([ortho, jnp.zeros((LANES - rank, keys), f32)], axis=0)
    turn = dot(summed, ortho_padded, 1, 0, highest)
    own_keys = base_keys - (outer_rate * (1.0 + outer_beta) * scale) * turn
    ga[z] = key_grad(own_keys, cotangent[...].astype(f32), gain[...]).astype(bf16)
    gather_ring(nz, z, ga, ss, rs, 10)
    last = pltpu.make_async_copy(ga, grads_at, ls.at[4])
    last.start()

    drain(pb, ss.at[0])
    drain(ps.at[pl.ds(0, chips - 1)], ss.at[1])
    drain(ps.at[pl.ds(0, chips - 1)], ss.at[2])
    drain(pb, ss.at[3])
    drain(lz.at[pl.ds(0, nz - 1)], ss.at[4])
    drain(ps.at[pl.ds(0, chips - 1)], ss.at[5])
    drain(kb.at[pl.ds(0, 13)], ss.at[13])
    drain(ks, ss.at[14])
    drain(pb, ss.at[7])
    drain(la.at[pl.ds(0, nr - 1)], ss.at[8])
    drain(pp.at[pl.ds(0, nz - 1)], ss.at[9])
    for store in stores:
        store.wait()
    last.wait()


def solution(mesh):
    nr, nz = mesh.shape["replica"], mesh.shape["tensor"]
    chips = nr // 2

    def body(tokens, cotangent, drift, error, weight, momentum, factor, gain):
        count, width = tokens.shape
        keys = drift.shape[1]
        rows = weight.shape[0]
        mine = count // nz
        scale = 1.0 / math.sqrt(width * nz)
        state = jax.ShapeDtypeStruct(weight.shape, f32)
        square = jax.ShapeDtypeStruct((keys, width), bf16)
        right = jax.ShapeDtypeStruct(factor.shape, f32)
        in_vmem = pl.BlockSpec(memory_space=pltpu.VMEM)
        in_hbm = pl.BlockSpec(memory_space=pltpu.HBM)
        held = pl.pallas_call(
            functools.partial(kernel, nr, nz, scale),
            out_shape=(
                state,
                state,
                square,
                right,
                jax.ShapeDtypeStruct((nz, mine, keys), bf16),
            ),
            in_specs=[in_hbm] * 8,
            out_specs=(in_hbm,) * 5,
            scratch_shapes=[
                pltpu.VMEM(weight.shape, f32),
                pltpu.VMEM(weight.shape, f32),
                pltpu.VMEM((keys, width), bf16),
                pltpu.VMEM(factor.shape, f32),
                pltpu.VMEM((nz, mine, keys), bf16),
                pltpu.VMEM(tokens.shape, bf16),
                pltpu.VMEM(cotangent.shape, bf16),
                pltpu.VMEM((keys, width), bf16),
                pltpu.VMEM((keys, width), bf16),
                pltpu.VMEM(weight.shape, f32),
                pltpu.VMEM(weight.shape, f32),
                pltpu.VMEM(factor.shape, f32),
                pltpu.VMEM((1, LANES), f32),
                pltpu.VMEM((chips, 2, rows, width), bf16),
                pltpu.VMEM((chips, rows, width), bf16),
                pltpu.VMEM((chips, rows, width), bf16),
                pltpu.VMEM((chips, rows, width), bf16),
                pltpu.VMEM((chips, 2, rows, width), bf16),
                pltpu.VMEM((chips, 2, rows, width), bf16),
                pltpu.VMEM((nz, GROUP, LANES), f32),
                pltpu.VMEM((nr, GROUP, LANES), f32),
                pltpu.VMEM((nr, rows, LANES), f32),
                pltpu.VMEM((nz, mine, keys), bf16),
                pltpu.VMEM((4, 3, mine, keys), bf16),
                pltpu.VMEM((2, mine // 2, keys), bf16),
                pltpu.VMEM((2, mine, keys), bf16),
                pltpu.VMEM((2, mine, keys), bf16),
                pltpu.VMEM((nz, GROUP, LANES), f32),
                pltpu.VMEM((nz, GROUP, LANES), f32),
                pltpu.SemaphoreType.DMA((15,)),
                pltpu.SemaphoreType.DMA((15,)),
                pltpu.SemaphoreType.DMA((8,)),
            ],
            compiler_params=pltpu.CompilerParams(
                collective_id=0, has_side_effects=True, vmem_limit_bytes=GRANT
            ),
            name="outer_inner_step",
        )(
            tokens, cotangent, drift[0], error[0], weight, momentum, factor, gain.reshape(1, -1)
        )
        out = pl.pallas_call(
            functools.partial(finish, scale),
            out_shape=(state, state, square, right, square),
            in_specs=[in_hbm] * 6,
            out_specs=(in_hbm,) * 5,
            scratch_shapes=[
                pltpu.VMEM(weight.shape, f32),
                pltpu.VMEM(weight.shape, f32),
                pltpu.VMEM((keys, width), bf16),
                pltpu.VMEM(factor.shape, f32),
                pltpu.VMEM((count, width), bf16),
                pltpu.VMEM((count, keys), bf16),
                pltpu.VMEM((2, keys // 2, width), bf16),
                pltpu.SemaphoreType.DMA((6,)),
                pltpu.SemaphoreType.DMA((6,)),
            ],
            compiler_params=pltpu.CompilerParams(vmem_limit_bytes=GRANT),
            name="weight_gradient",
        )(*held[:4], tokens, held[4].reshape(count, keys))
        return (out[0], out[1], out[2][None], out[3], out[4][None])

    placed = (
        P("replica", "tensor"),
        P(("replica", "tensor"), None),
        P("replica", None, "tensor"),
        P("replica", None, "tensor"),
        P("replica", "tensor"),
        P("replica", "tensor"),
        P(None, "tensor"),
        P(),
    )
    return jax.shard_map(
        body,
        mesh=mesh,
        in_specs=placed,
        out_specs=(
            P("replica", "tensor"),
            P("replica", "tensor"),
            P("replica", None, "tensor"),
            P(None, "tensor"),
            P("replica", None, "tensor"),
        ),
        check_vma=False,
    )
```

```python
import functools
import math

import jax
import jax.numpy as jnp
from jax import lax
from jax.experimental import pallas as pl
from jax.experimental.pallas import tpu as pltpu
from jax.sharding import PartitionSpec as P

MESH = pl.DeviceIdType.MESH
highest = lax.Precision.HIGHEST
f32 = jnp.float32
bf16 = jnp.bfloat16
outer_rate = 0.7
outer_beta = 0.9
LANES = 128
GROUP = 8
GRANT = 60 * 1024 * 1024


def dot(left, right, left_dim, right_dim, precision=None):
    return lax.dot_general(
        left,
        right,
        (((left_dim,), (right_dim,)), ((), ())),
        precision=precision,
        preferred_element_type=f32,
    )


def split_dot(left, right, left_dim, right_dim):
    high = left.astype(bf16)
    low = (left - high.astype(f32)).astype(bf16)
    return dot(high, right, left_dim, right_dim) + dot(low, right, left_dim, right_dim)


def send(src, dst, send_sem, recv_sem, device):
    pltpu.make_async_remote_copy(
        src_ref=src,
        dst_ref=dst,
        send_sem=send_sem,
        recv_sem=recv_sem,
        device_id=device,
        device_id_type=MESH,
    ).start()


def drain(ref, sem):
    pltpu.make_async_copy(ref, ref, sem).wait()


def each_other(count, me, act):
    def step(i, carry):
        half = (i + 1) // 2
        offset = count // 2 + half * (2 * (i % 2) - 1)
        act(lax.rem(me + offset, count))
        return carry

    lax.fori_loop(0, count - 1, step, 0, unroll=True)


def pack(rows, rank):
    groups = rows.shape[1] // GROUP
    total = rows[:, 0:GROUP]
    for g in range(1, groups):
        total = total + pltpu.roll(rows[:, g * GROUP : (g + 1) * GROUP], g * rank, 2)
    return total


def unpack(packed, groups, rank):
    lane = lax.broadcasted_iota(jnp.int32, packed.shape, 2)
    parts = []
    for g in range(groups):
        turned = packed if g == 0 else pltpu.roll(packed, LANES - g * rank, 2)
        parts.append(jnp.where(lane < rank, turned, 0.0))
    return jnp.concatenate(parts, axis=1)


def fold(packed):
    turned = pltpu.roll(pltpu.roll(packed, LANES // 2, 2), GROUP // 2, 1)
    return (packed + turned)[:, 0 : GROUP // 2]


def unfold(folded):
    return jnp.concatenate([folded, pltpu.roll(folded, LANES // 2, 2)], axis=1)


def inverse_factor(gram, rank):
    row = lax.broadcasted_iota(jnp.int32, (rank, LANES), 0)
    lane = lax.broadcasted_iota(jnp.int32, (rank, LANES), 1)
    diagonal = row == lane
    trace = jnp.sum(
        jnp.sum(jnp.where(diagonal, gram, 0.0), axis=1, keepdims=True), axis=0, keepdims=True
    )
    shift = 0.001 * trace / rank + 1e-06
    a = jnp.where(lane < rank, gram, 0.0) + jnp.where(diagonal, shift, 0.0)
    a = a + jnp.where(lane == row + rank, 1.0, 0.0)
    down = lax.broadcasted_iota(jnp.int32, (rank, 1), 0)
    for k in range(rank - 1):
        pivot_row = a[k : k + 1, :]
        share = pivot_row * (1.0 / pivot_row[:, k : k + 1])
        column = jnp.where(down > k, a[:, k : k + 1], 0.0)
        a = a - column * share
    pivots = jnp.sum(jnp.where(diagonal, a, 0.0), axis=1, keepdims=True)
    a = a * (1.0 / jnp.sqrt(pivots))
    return jnp.where(lane < rank, pltpu.roll(a, LANES - rank, 1), 0.0)


def key_grad(keys, cotangent, gain):
    width = gain.shape[1]
    parts = []
    for head in range(keys.shape[1] // width):
        at = slice(head * width, (head + 1) * width)
        shaped = keys[:, at]
        weighted = gain * cotangent[:, at]
        inverse = lax.rsqrt(jnp.mean(shaped * shaped, axis=1, keepdims=True) + 1e-06)
        inner = jnp.sum(weighted * shaped, axis=1, keepdims=True)
        parts.append(
            weighted * inverse - shaped * (inverse * inverse * inverse * inner / width)
        )
    return jnp.concatenate(parts, axis=1)


def gather_ring(count, me, ga, ss, rs, at):
    half = ga.shape[1] // 2

    def peer(offset):
        return {"tensor": lax.rem(me + offset + count, count)}

    def block(offset):
        return ga.at[lax.rem(me + offset + count, count)]

    near = at + 2
    send(block(0), block(0), ss.at[at], rs.at[at], peer(5))
    send(block(0), block(0), ss.at[at + 1], rs.at[at + 1], peer(-5))
    for offset in (2, -2, 1, -1):
        send(block(0), block(0), ss.at[near], rs.at[near], peer(offset))
    drain(block(0), rs.at[at])
    low = block(-5).at[pl.ds(0, half)]
    send(low, low, ss.at[near], rs.at[near], peer(3))
    for offset in (2, -2, 1, -1):
        send(block(-5), block(-5), ss.at[near], rs.at[near], peer(offset))
    drain(block(0), rs.at[at + 1])
    high = block(5).at[pl.ds(half, half)]
    send(high, high, ss.at[near], rs.at[near], peer(-3))
    for offset in (2, -2, 1, -1):
        send(block(5), block(5), ss.at[near], rs.at[near], peer(offset))
    drain(ga.at[pl.ds(0, 13)], rs.at[near])
    drain(block(0), ss.at[at])
    drain(block(0), ss.at[at + 1])
    drain(ga.at[pl.ds(0, 13)], ss.at[near])


def scatter_near(count, me, kb, kn, kh, ss, rs, at):
    half = kb.shape[1] // 2

    def index(offset):
        return lax.rem(me + offset + 2 * count, count)

    for far, offset in ((5, 3), (-5, -3)):
        side = 0 if far > 0 else 1
        send(
            kb.at[index(offset + far), pl.ds(side * half, half)], kh.at[side],
            ss.at[at], rs.at[at], {"tensor": index(offset)},
        )
    for i, far in enumerate((5, -5, 0)):
        for j, offset in enumerate((2, -2, 1, -1)):
            send(
                kb.at[index(offset + far)], kn.at[j, i],
                ss.at[at], rs.at[at], {"tensor": index(offset)},
            )


def scatter_far(count, me, kb, kn, kh, ks, kr, ss, rs, at):
    half = kb.shape[1] // 2

    def index(offset):
        return lax.rem(me + offset + 2 * count, count)

    drain(kb.at[pl.ds(0, 13)], rs.at[at])
    for i, far in enumerate((5, -5)):
        total = kb[index(far)].astype(f32)
        for j in range(4):
            total = total + kn[j, i].astype(f32)
        eighth = kh[i].astype(f32)
        blank = jnp.zeros_like(eighth)
        total = total + jnp.concatenate([eighth, blank] if i == 0 else [blank, eighth], axis=0)
        ks[i] = total.astype(bf16)
        send(ks.at[i], kr.at[i], ss.at[at + 1], rs.at[at + 1], {"tensor": index(far)})
    total = kb[me].astype(f32)
    for j in range(4):
        total = total + kn[j, 2].astype(f32)
    return total


def finish(
    scale, nw_at, nm_at, ne_at, nf_at, tokens_at, grads_at,
    nw_out, nm_out, ne_out, nf_out, wg_out,
    nw, nm, ne, nf, tokens, grads, held, in_sems, out_sems,
):
    pairs = (
        (grads_at, grads), (tokens_at, tokens),
        (ne_at, ne), (nf_at, nf), (nw_at, nw), (nm_at, nm),
    )
    ins = [pltpu.make_async_copy(src, dst, in_sems.at[i]) for i, (src, dst) in enumerate(pairs)]
    for copy in ins:
        copy.start()
    outs = []

    def leave(src, dst):
        outs.append(pltpu.make_async_copy(src, dst, out_sems.at[len(outs)]))
        outs[-1].start()

    ins[0].wait()
    ins[1].wait()
    half = held.shape[1]
    for i in range(2):
        left = grads[:, i * half : (i + 1) * half]
        held[i] = (dot(left, tokens[...], 0, 0) * scale).astype(bf16)
        leave(held.at[i], wg_out.at[pl.ds(i * half, half)])
        if i == 0:
            results = ((ne, ne_out), (nf, nf_out), (nw, nw_out), (nm, nm_out))
            for load, (src, dst) in zip(ins[2:], results):
                load.wait()
                leave(src, dst)
    for copy in outs:
        copy.wait()


def kernel(
    nr, nz, scale,
    tokens_at, cotangent_at, drift_at, error_at, weight_at, momentum_at, factor_at, gain_at,
    new_weight_at, new_momentum_at, new_error_at, new_factor_at, grads_at,
    new_weight, new_momentum, new_error, new_factor, ga,
    tokens, cotangent, drift, error, weight, momentum, factor, gain,
    mb, pb, ps, mr, ub, mg, lp, lq, lz, la, lt, kb, kn, kh, ks, kr, pp, pr, ss, rs, ls,
):
    r = lax.axis_index("replica")
    z = lax.axis_index("tensor")
    chips = nr // 2
    chip, core = r // 2, lax.rem(r, 2)
    other = 1 - core
    partner = {"replica": chip * 2 + other}
    rank, width = factor.shape
    keys = drift.shape[0]
    rows = weight.shape[0]
    mine = tokens.shape[0] // nz

    def across(chip_at):
        return {"replica": chip_at * 2 + core}

    loads = [
        pltpu.make_async_copy(src, dst, ls.at[i])
        for i, (src, dst) in enumerate(
            (
                (drift_at, drift),
                (error_at, error),
                (weight_at, weight),
                (momentum_at, momentum),
                (factor_at, factor),
                (tokens_at, tokens),
                (cotangent_at, cotangent),
                (gain_at, gain),
            )
        )
    ]
    for load in loads[:4]:
        load.start()
    barrier = pltpu.get_barrier_semaphore()

    def greet_replica(peer):
        pl.semaphore_signal(barrier, inc=1, device_id={"replica": peer}, device_id_type=MESH)

    def greet_tensor(peer):
        pl.semaphore_signal(barrier, inc=1, device_id={"tensor": peer}, device_id_type=MESH)

    each_other(nz, z, greet_tensor)
    each_other(nr, r, greet_replica)
    for load in loads[4:]:
        load.start()
    for load in loads[:4]:
        load.wait()

    merged = drift[...].astype(f32) + error[...].astype(f32)
    mb[...] = merged.astype(bf16).reshape(mb.shape)
    base = weight[...] - (outer_rate * outer_beta * outer_beta) * momentum[...]
    ub[chip, core] = base.astype(bf16)
    for load in loads[4:]:
        load.wait()
    padded = jnp.concatenate([factor[...], jnp.zeros((LANES - rank, width), f32)], axis=0)
    term = dot(merged, padded, 1, 1, highest) * (1.0 / nr)
    lp[...] = fold(pack(term.reshape(nr, rows, LANES), rank))
    pl.semaphore_wait(barrier, nr + nz - 2)

    each_other(
        nr, r,
        lambda p: send(lp.at[p], lq.at[r], ss.at[15], rs.at[15], {"replica": p}),
    )
    lq[r] = lp[r]

    send(mb.at[:, other], pb, ss.at[0], rs.at[0], partner)
    each_other(
        chips, chip,
        lambda p: send(ub.at[chip, core], ub.at[chip, core], ss.at[1], rs.at[1], across(p)),
    )
    drain(pb, rs.at[0])
    ps[...] = (mb[:, pl.ds(core, 1)][:, 0].astype(f32) + pb[...].astype(f32)).astype(bf16)
    each_other(
        chips, chip,
        lambda p: send(ps.at[p], mr.at[chip], ss.at[2], rs.at[2], across(p)),
    )
    mr[chip] = ps[chip]

    drain(lq.at[pl.ds(0, nr - 1)], rs.at[15])
    lz[z] = jnp.sum(lq[...], axis=0)
    each_other(
        nz, z,
        lambda p: send(lz.at[z], lz.at[z], ss.at[4], rs.at[4], {"tensor": p}),
    )

    drain(ps.at[pl.ds(0, chips - 1)], rs.at[1])
    send(ub.at[:, core], ub.at[:, core], ss.at[3], rs.at[3], partner)
    drain(ps.at[pl.ds(0, chips - 1)], rs.at[2])
    mean = jnp.sum(mr[...].astype(f32), axis=0) * (1.0 / nr)
    mg[chip, core] = mean.astype(bf16)
    each_other(
        chips, chip,
        lambda p: send(mg.at[chip, core], mg.at[chip, core], ss.at[5], rs.at[5], across(p)),
    )

    drain(pb, rs.at[3])
    partial = dot(tokens[...], ub[...].reshape(keys, width), 1, 1) * scale
    kb[...] = partial.astype(bf16).reshape(kb.shape)
    scatter_near(nz, z, kb, kn, kh, ss, rs, 13)

    drain(lz.at[pl.ds(0, nz - 1)], rs.at[4])
    la[r] = jnp.sum(lz[...], axis=0)
    each_other(
        nr, r,
        lambda p: send(la.at[r], la.at[r], ss.at[8], rs.at[8], {"replica": p}),
    )
    drain(ps.at[pl.ds(0, chips - 1)], rs.at[5])
    send(mg.at[:, core], mg.at[:, core], ss.at[7], rs.at[7], partner)
    near_keys = scatter_far(nz, z, kb, kn, kh, ks, kr, ss, rs, 13)
    drain(pb, rs.at[7])
    drain(la.at[pl.ds(0, nr - 1)], rs.at[8])
    left = unpack(unfold(la[...]), rows // GROUP, rank)
    lt[...] = left.reshape(lt.shape)
    left = left.reshape(keys, LANES)
    gram = dot(left, left, 0, 0, highest)[0:rank]
    inverse = inverse_factor(gram, rank)
    ortho = dot(inverse, left, 1, 1, highest)
    right = split_dot(ortho, mg[...].reshape(keys, width), 1, 0)
    new_factor[...] = right
    zeros = jnp.zeros((LANES - rank, width), f32)
    right_padded = jnp.concatenate([right, zeros], axis=0)
    product = dot(tokens[...], right_padded.astype(bf16), 1, 1)
    pp[...] = pack(product.reshape(nz, mine, LANES), rank)
    each_other(
        nz, z,
        lambda p: send(pp.at[p], pr.at[z], ss.at[9], rs.at[9], {"tensor": p}),
    )
    pr[z] = pp[z]

    inverse_padded = jnp.concatenate([inverse, jnp.zeros((LANES - rank, LANES), f32)], axis=0)
    own_ortho = dot(lt[r], inverse_padded, 1, 1, highest)
    own_approx = dot(own_ortho, right_padded, 1, 0, highest)
    next_momentum = outer_beta * momentum[...] + own_approx
    new_momentum[...] = next_momentum
    new_weight[...] = weight[...] - outer_rate * (own_approx + outer_beta * next_momentum)
    ortho_rows = dot(left, inverse_padded, 1, 1).astype(bf16)
    approx = dot(ortho_rows, right_padded.astype(bf16), 1, 0)
    new_error[...] = (merged - approx).astype(bf16)

    stores = [
        pltpu.make_async_copy(src, dst, ls.at[i])
        for i, (src, dst) in enumerate(
            (
                (new_error, new_error_at),
                (new_factor, new_factor_at),
                (new_weight, new_weight_at),
                (new_momentum, new_momentum_at),
            )
        )
    ]
    for store in stores:
        store.start()

    drain(kr, rs.at[14])
    base_keys = near_keys + kr[0].astype(f32) + kr[1].astype(f32)
    drain(pp.at[pl.ds(0, nz - 1)], rs.at[9])
    summed = unpack(jnp.sum(pr[...], axis=0)[None], mine // GROUP, rank)[0]
    ortho_padded = jnp.concatenate([ortho, jnp.zeros((LANES - rank, keys), f32)], axis=0)
    turn = dot(summed, ortho_padded, 1, 0, highest)
    own_keys = base_keys - (outer_rate * (1.0 + outer_beta) * scale) * turn
    ga[z] = key_grad(own_keys, cotangent[...].astype(f32), gain[...]).astype(bf16)
    gather_ring(nz, z, ga, ss, rs, 10)
    last = pltpu.make_async_copy(ga, grads_at, ls.at[4])
    last.start()

    drain(pb, ss.at[0])
    drain(ps.at[pl.ds(0, chips - 1)], ss.at[1])
    drain(ps.at[pl.ds(0, chips - 1)], ss.at[2])
    drain(pb, ss.at[3])
    drain(lz.at[pl.ds(0, nz - 1)], ss.at[4])
    drain(ps.at[pl.ds(0, chips - 1)], ss.at[5])
    drain(kb.at[pl.ds(0, 13)], ss.at[13])
    drain(ks, ss.at[14])
    drain(pb, ss.at[7])
    drain(la.at[pl.ds(0, nr - 1)], ss.at[8])
    drain(lq.at[pl.ds(0, nr - 1)], ss.at[15])
    drain(pp.at[pl.ds(0, nz - 1)], ss.at[9])
    for store in stores:
        store.wait()
    last.wait()


def solution(mesh):
    nr, nz = mesh.shape["replica"], mesh.shape["tensor"]
    chips = nr // 2

    def body(tokens, cotangent, drift, error, weight, momentum, factor, gain):
        count, width = tokens.shape
        keys = drift.shape[1]
        rows = weight.shape[0]
        mine = count // nz
        scale = 1.0 / math.sqrt(width * nz)
        state = jax.ShapeDtypeStruct(weight.shape, f32)
        square = jax.ShapeDtypeStruct((keys, width), bf16)
        right = jax.ShapeDtypeStruct(factor.shape, f32)
        in_vmem = pl.BlockSpec(memory_space=pltpu.VMEM)
        in_hbm = pl.BlockSpec(memory_space=pltpu.HBM)
        held = pl.pallas_call(
            functools.partial(kernel, nr, nz, scale),
            out_shape=(
                state,
                state,
                square,
                right,
                jax.ShapeDtypeStruct((nz, mine, keys), bf16),
            ),
            in_specs=[in_hbm] * 8,
            out_specs=(in_hbm,) * 5,
            scratch_shapes=[
                pltpu.VMEM(weight.shape, f32),
                pltpu.VMEM(weight.shape, f32),
                pltpu.VMEM((keys, width), bf16),
                pltpu.VMEM(factor.shape, f32),
                pltpu.VMEM((nz, mine, keys), bf16),
                pltpu.VMEM(tokens.shape, bf16),
                pltpu.VMEM(cotangent.shape, bf16),
                pltpu.VMEM((keys, width), bf16),
                pltpu.VMEM((keys, width), bf16),
                pltpu.VMEM(weight.shape, f32),
                pltpu.VMEM(weight.shape, f32),
                pltpu.VMEM(factor.shape, f32),
                pltpu.VMEM((1, LANES), f32),
                pltpu.VMEM((chips, 2, rows, width), bf16),
                pltpu.VMEM((chips, rows, width), bf16),
                pltpu.VMEM((chips, rows, width), bf16),
                pltpu.VMEM((chips, rows, width), bf16),
                pltpu.VMEM((chips, 2, rows, width), bf16),
                pltpu.VMEM((chips, 2, rows, width), bf16),
                pltpu.VMEM((nr, GROUP // 2, LANES), f32),
                pltpu.VMEM((nr, GROUP // 2, LANES), f32),
                pltpu.VMEM((nz, GROUP // 2, LANES), f32),
                pltpu.VMEM((nr, GROUP // 2, LANES), f32),
                pltpu.VMEM((nr, rows, LANES), f32),
                pltpu.VMEM((nz, mine, keys), bf16),
                pltpu.VMEM((4, 3, mine, keys), bf16),
                pltpu.VMEM((2, mine // 2, keys), bf16),
                pltpu.VMEM((2, mine, keys), bf16),
                pltpu.VMEM((2, mine, keys), bf16),
                pltpu.VMEM((nz, GROUP, LANES), f32),
                pltpu.VMEM((nz, GROUP, LANES), f32),
                pltpu.SemaphoreType.DMA((16,)),
                pltpu.SemaphoreType.DMA((16,)),
                pltpu.SemaphoreType.DMA((8,)),
            ],
            compiler_params=pltpu.CompilerParams(
                collective_id=0, has_side_effects=True, vmem_limit_bytes=GRANT
            ),
            name="outer_inner_step",
        )(
            tokens, cotangent, drift[0], error[0], weight, momentum, factor, gain.reshape(1, -1)
        )
        out = pl.pallas_call(
            functools.partial(finish, scale),
            out_shape=(state, state, square, right, square),
            in_specs=[in_hbm] * 6,
            out_specs=(in_hbm,) * 5,
            scratch_shapes=[
                pltpu.VMEM(weight.shape, f32),
                pltpu.VMEM(weight.shape, f32),
                pltpu.VMEM((keys, width), bf16),
                pltpu.VMEM(factor.shape, f32),
                pltpu.VMEM((count, width), bf16),
                pltpu.VMEM((count, keys), bf16),
                pltpu.VMEM((2, keys // 2, width), bf16),
                pltpu.SemaphoreType.DMA((6,)),
                pltpu.SemaphoreType.DMA((6,)),
            ],
            compiler_params=pltpu.CompilerParams(vmem_limit_bytes=GRANT),
            name="weight_gradient",
        )(*held[:4], tokens, held[4].reshape(count, keys))
        return (out[0], out[1], out[2][None], out[3], out[4][None])

    placed = (
        P("replica", "tensor"),
        P(("replica", "tensor"), None),
        P("replica", None, "tensor"),
        P("replica", None, "tensor"),
        P("replica", "tensor"),
        P("replica", "tensor"),
        P(None, "tensor"),
        P(),
    )
    return jax.shard_map(
        body,
        mesh=mesh,
        in_specs=placed,
        out_specs=(
            P("replica", "tensor"),
            P("replica", "tensor"),
            P("replica", None, "tensor"),
            P(None, "tensor"),
            P("replica", None, "tensor"),
        ),
        check_vma=False,
    )
```

```python
import functools
import math

import jax
import jax.numpy as jnp
from jax import lax
from jax.experimental import pallas as pl
from jax.experimental.pallas import tpu as pltpu
from jax.sharding import PartitionSpec as P

MESH = pl.DeviceIdType.MESH
highest = lax.Precision.HIGHEST
f32 = jnp.float32
bf16 = jnp.bfloat16
outer_rate = 0.7
outer_beta = 0.9
LANES = 128
GROUP = 8
GRANT = 60 * 1024 * 1024


def dot(left, right, left_dim, right_dim, precision=None):
    return lax.dot_general(
        left,
        right,
        (((left_dim,), (right_dim,)), ((), ())),
        precision=precision,
        preferred_element_type=f32,
    )


def split_dot(left, right, left_dim, right_dim):
    high = left.astype(bf16)
    low = (left - high.astype(f32)).astype(bf16)
    return dot(high, right, left_dim, right_dim) + dot(low, right, left_dim, right_dim)


def send(src, dst, send_sem, recv_sem, device):
    pltpu.make_async_remote_copy(
        src_ref=src,
        dst_ref=dst,
        send_sem=send_sem,
        recv_sem=recv_sem,
        device_id=device,
        device_id_type=MESH,
    ).start()


def drain(ref, sem):
    pltpu.make_async_copy(ref, ref, sem).wait()


def each_other(count, me, act):
    def step(i, carry):
        half = (i + 1) // 2
        offset = count // 2 + half * (2 * (i % 2) - 1)
        act(lax.rem(me + offset, count))
        return carry

    lax.fori_loop(0, count - 1, step, 0, unroll=True)


def pack(rows, rank):
    groups = rows.shape[1] // GROUP
    total = rows[:, 0:GROUP]
    for g in range(1, groups):
        total = total + pltpu.roll(rows[:, g * GROUP : (g + 1) * GROUP], g * rank, 2)
    return total


def unpack(packed, groups, rank):
    lane = lax.broadcasted_iota(jnp.int32, packed.shape, 2)
    parts = []
    for g in range(groups):
        turned = packed if g == 0 else pltpu.roll(packed, LANES - g * rank, 2)
        parts.append(jnp.where(lane < rank, turned, 0.0))
    return jnp.concatenate(parts, axis=1)


def fold(packed):
    turned = pltpu.roll(pltpu.roll(packed, LANES // 2, 2), GROUP // 2, 1)
    return (packed + turned)[:, 0 : GROUP // 2]


def unfold(folded):
    return jnp.concatenate([folded, pltpu.roll(folded, LANES // 2, 2)], axis=1)


def inverse_factor(gram, rank):
    row = lax.broadcasted_iota(jnp.int32, (rank, LANES), 0)
    lane = lax.broadcasted_iota(jnp.int32, (rank, LANES), 1)
    diagonal = row == lane
    trace = jnp.sum(
        jnp.sum(jnp.where(diagonal, gram, 0.0), axis=1, keepdims=True), axis=0, keepdims=True
    )
    shift = 0.001 * trace / rank + 1e-06
    a = jnp.where(lane < rank, gram, 0.0) + jnp.where(diagonal, shift, 0.0)
    a = a + jnp.where(lane == row + rank, 1.0, 0.0)
    down = lax.broadcasted_iota(jnp.int32, (rank, 1), 0)
    for k in range(0, rank, 2):
        first, second = a[k : k + 1, :], a[k + 1 : k + 2, :]
        corner, cross, last = first[:, k : k + 1], first[:, k + 1 : k + 2], second[:, k + 1 : k + 2]
        scaled = 1.0 / corner
        ratio = cross * scaled
        share = 1.0 / (last - cross * ratio)
        second = second - ratio * first
        near = jnp.where(down > k, a[:, k : k + 1], 0.0)
        far = jnp.where(down > k + 1, a[:, k + 1 : k + 2] - ratio * near, 0.0)
        a = a - near * (first * scaled) - far * (second * share)
    pivots = jnp.sum(jnp.where(diagonal, a, 0.0), axis=1, keepdims=True)
    a = a * (1.0 / jnp.sqrt(pivots))
    return jnp.where(lane < rank, pltpu.roll(a, LANES - rank, 1), 0.0)


def key_grad(keys, cotangent, gain):
    width = gain.shape[1]
    parts = []
    for head in range(keys.shape[1] // width):
        at = slice(head * width, (head + 1) * width)
        shaped = keys[:, at]
        weighted = gain * cotangent[:, at]
        inverse = lax.rsqrt(jnp.mean(shaped * shaped, axis=1, keepdims=True) + 1e-06)
        inner = jnp.sum(weighted * shaped, axis=1, keepdims=True)
        parts.append(
            weighted * inverse - shaped * (inverse * inverse * inverse * inner / width)
        )
    return jnp.concatenate(parts, axis=1)


def gather_ring(count, me, ga, ss, rs, at):
    half = ga.shape[1] // 2

    def peer(offset):
        return {"tensor": lax.rem(me + offset + count, count)}

    def block(offset):
        return ga.at[lax.rem(me + offset + count, count)]

    near = at + 2
    send(block(0), block(0), ss.at[at], rs.at[at], peer(5))
    send(block(0), block(0), ss.at[at + 1], rs.at[at + 1], peer(-5))
    for offset in (2, -2, 1, -1):
        send(block(0), block(0), ss.at[near], rs.at[near], peer(offset))
    drain(block(0), rs.at[at])
    low = block(-5).at[pl.ds(0, half)]
    send(low, low, ss.at[near], rs.at[near], peer(3))
    for offset in (2, -2, 1, -1):
        send(block(-5), block(-5), ss.at[near], rs.at[near], peer(offset))
    drain(block(0), rs.at[at + 1])
    high = block(5).at[pl.ds(half, half)]
    send(high, high, ss.at[near], rs.at[near], peer(-3))
    for offset in (2, -2, 1, -1):
        send(block(5), block(5), ss.at[near], rs.at[near], peer(offset))
    drain(ga.at[pl.ds(0, 13)], rs.at[near])
    drain(block(0), ss.at[at])
    drain(block(0), ss.at[at + 1])
    drain(ga.at[pl.ds(0, 13)], ss.at[near])


def scatter_near(count, me, kb, kn, kh, ss, rs, at):
    half = kb.shape[1] // 2

    def index(offset):
        return lax.rem(me + offset + 2 * count, count)

    for far, offset in ((5, 3), (-5, -3)):
        side = 0 if far > 0 else 1
        send(
            kb.at[index(offset + far), pl.ds(side * half, half)], kh.at[side],
            ss.at[at], rs.at[at], {"tensor": index(offset)},
        )
    for i, far in enumerate((5, -5)):
        for j, offset in enumerate((2, -2, 1, -1)):
            send(
                kb.at[index(offset + far)], kn.at[j, i],
                ss.at[at], rs.at[at], {"tensor": index(offset)},
            )


def scatter_far(count, me, kb, kn, kh, ks, kr, ss, rs, at):
    half = kb.shape[1] // 2

    def index(offset):
        return lax.rem(me + offset + 2 * count, count)

    drain(kb.at[pl.ds(0, 9)], rs.at[at])
    for i, far in enumerate((5, -5)):
        total = kb[index(far)].astype(f32)
        for j in range(4):
            total = total + kn[j, i].astype(f32)
        eighth = kh[i].astype(f32)
        blank = jnp.zeros_like(eighth)
        total = total + jnp.concatenate([eighth, blank] if i == 0 else [blank, eighth], axis=0)
        ks[i] = total.astype(bf16)
        send(ks.at[i], kr.at[i], ss.at[at + 1], rs.at[at + 1], {"tensor": index(far)})
    for j, offset in enumerate((2, -2, 1, -1)):
        send(
            kb.at[index(offset)], kn.at[j, 2],
            ss.at[at], rs.at[at + 3], {"tensor": index(offset)},
        )


def finish(
    scale, nw_at, nm_at, ne_at, nf_at, tokens_at, grads_at,
    nw_out, nm_out, ne_out, nf_out, wg_out,
    nw, nm, ne, nf, tokens, grads, held, in_sems, out_sems,
):
    pairs = (
        (grads_at, grads), (tokens_at, tokens),
        (ne_at, ne), (nf_at, nf), (nw_at, nw), (nm_at, nm),
    )
    ins = [pltpu.make_async_copy(src, dst, in_sems.at[i]) for i, (src, dst) in enumerate(pairs)]
    for copy in ins:
        copy.start()
    outs = []

    def leave(src, dst):
        outs.append(pltpu.make_async_copy(src, dst, out_sems.at[len(outs)]))
        outs[-1].start()

    ins[0].wait()
    ins[1].wait()
    half = held.shape[1]
    for i in range(2):
        left = grads[:, i * half : (i + 1) * half]
        held[i] = (dot(left, tokens[...], 0, 0) * scale).astype(bf16)
        leave(held.at[i], wg_out.at[pl.ds(i * half, half)])
        if i == 0:
            results = ((ne, ne_out), (nf, nf_out), (nw, nw_out), (nm, nm_out))
            for load, (src, dst) in zip(ins[2:], results):
                load.wait()
                leave(src, dst)
    for copy in outs:
        copy.wait()


def kernel(
    nr, nz, scale,
    tokens_at, cotangent_at, drift_at, error_at, weight_at, momentum_at, factor_at, gain_at,
    new_weight_at, new_momentum_at, new_error_at, new_factor_at, grads_at,
    new_weight, new_momentum, new_error, new_factor, ga,
    tokens, cotangent, drift, error, weight, momentum, factor, gain,
    mb, pb, ps, mr, ub, mg, lp, lq, lz, la, lt, kb, kn, kh, ks, kr, pp, pr, ss, rs, ls,
):
    r = lax.axis_index("replica")
    z = lax.axis_index("tensor")
    chips = nr // 2
    chip, core = r // 2, lax.rem(r, 2)
    other = 1 - core
    partner = {"replica": chip * 2 + other}
    rank, width = factor.shape
    keys = drift.shape[0]
    rows = weight.shape[0]
    mine = tokens.shape[0] // nz

    def across(chip_at):
        return {"replica": chip_at * 2 + core}

    loads = [
        pltpu.make_async_copy(src, dst, ls.at[i])
        for i, (src, dst) in enumerate(
            (
                (drift_at, drift),
                (error_at, error),
                (weight_at, weight),
                (momentum_at, momentum),
                (factor_at, factor),
                (tokens_at, tokens),
                (cotangent_at, cotangent),
                (gain_at, gain),
            )
        )
    ]
    for load in loads[:4]:
        load.start()
    barrier = pltpu.get_barrier_semaphore()

    def greet_replica(peer):
        pl.semaphore_signal(barrier, inc=1, device_id={"replica": peer}, device_id_type=MESH)

    def greet_tensor(peer):
        pl.semaphore_signal(barrier, inc=1, device_id={"tensor": peer}, device_id_type=MESH)

    each_other(nz, z, greet_tensor)
    each_other(nr, r, greet_replica)
    for load in loads[4:]:
        load.start()
    for load in loads[:4]:
        load.wait()

    merged = drift[...].astype(f32) + error[...].astype(f32)
    mb[...] = merged.astype(bf16).reshape(mb.shape)
    base = weight[...] - (outer_rate * outer_beta * outer_beta) * momentum[...]
    ub[chip, core] = base.astype(bf16)
    for load in loads[4:]:
        load.wait()
    padded = jnp.concatenate([factor[...], jnp.zeros((LANES - rank, width), f32)], axis=0)
    term = dot(merged, padded, 1, 1, highest) * (1.0 / nr)
    lp[...] = fold(pack(term.reshape(nr, rows, LANES), rank))
    pl.semaphore_wait(barrier, nr + nz - 2)

    each_other(
        nr, r,
        lambda p: send(lp.at[p], lq.at[r], ss.at[15], rs.at[15], {"replica": p}),
    )
    lq[r] = lp[r]

    send(mb.at[:, other], pb, ss.at[0], rs.at[0], partner)
    each_other(
        chips, chip,
        lambda p: send(ub.at[chip, core], ub.at[chip, core], ss.at[1], rs.at[1], across(p)),
    )
    drain(pb, rs.at[0])
    ps[...] = (mb[:, pl.ds(core, 1)][:, 0].astype(f32) + pb[...].astype(f32)).astype(bf16)
    each_other(
        chips, chip,
        lambda p: send(ps.at[p], mr.at[chip], ss.at[2], rs.at[2], across(p)),
    )
    mr[chip] = ps[chip]

    drain(lq.at[pl.ds(0, nr - 1)], rs.at[15])
    lz[z] = jnp.sum(lq[...], axis=0)
    each_other(
        nz, z,
        lambda p: send(lz.at[z], lz.at[z], ss.at[4], rs.at[4], {"tensor": p}),
    )

    drain(ps.at[pl.ds(0, chips - 1)], rs.at[1])
    send(ub.at[:, core], ub.at[:, core], ss.at[3], rs.at[3], partner)
    drain(ps.at[pl.ds(0, chips - 1)], rs.at[2])
    mean = jnp.sum(mr[...].astype(f32), axis=0) * (1.0 / nr)
    mg[chip, core] = mean.astype(bf16)
    each_other(
        chips, chip,
        lambda p: send(mg.at[chip, core], mg.at[chip, core], ss.at[5], rs.at[5], across(p)),
    )

    drain(pb, rs.at[3])
    partial = dot(tokens[...], ub[...].reshape(keys, width), 1, 1) * scale
    kb[...] = partial.astype(bf16).reshape(kb.shape)
    scatter_near(nz, z, kb, kn, kh, ss, rs, 13)

    drain(lz.at[pl.ds(0, nz - 1)], rs.at[4])
    la[r] = jnp.sum(lz[...], axis=0)
    each_other(
        nr, r,
        lambda p: send(la.at[r], la.at[r], ss.at[8], rs.at[8], {"replica": p}),
    )
    drain(ps.at[pl.ds(0, chips - 1)], rs.at[5])
    send(mg.at[:, core], mg.at[:, core], ss.at[7], rs.at[7], partner)
    scatter_far(nz, z, kb, kn, kh, ks, kr, ss, rs, 13)
    drain(pb, rs.at[7])
    drain(la.at[pl.ds(0, nr - 1)], rs.at[8])
    left = unpack(unfold(la[...]), rows // GROUP, rank)
    lt[...] = left.reshape(lt.shape)
    left = left.reshape(keys, LANES)
    gram = dot(left, left, 0, 0, highest)[0:rank]
    inverse = inverse_factor(gram, rank)
    ortho = dot(inverse, left, 1, 1, highest)
    right = split_dot(ortho, mg[...].reshape(keys, width), 1, 0)
    new_factor[...] = right
    zeros = jnp.zeros((LANES - rank, width), f32)
    right_padded = jnp.concatenate([right, zeros], axis=0)
    product = dot(tokens[...], right_padded.astype(bf16), 1, 1)
    pp[...] = pack(product.reshape(nz, mine, LANES), rank)
    each_other(
        nz, z,
        lambda p: send(pp.at[p], pr.at[z], ss.at[9], rs.at[9], {"tensor": p}),
    )
    pr[z] = pp[z]

    inverse_padded = jnp.concatenate([inverse, jnp.zeros((LANES - rank, LANES), f32)], axis=0)
    own_ortho = dot(lt[r], inverse_padded, 1, 1, highest)
    own_approx = dot(own_ortho, right_padded, 1, 0, highest)
    next_momentum = outer_beta * momentum[...] + own_approx
    new_momentum[...] = next_momentum
    new_weight[...] = weight[...] - outer_rate * (own_approx + outer_beta * next_momentum)
    ortho_rows = dot(left, inverse_padded, 1, 1).astype(bf16)
    approx = dot(ortho_rows, right_padded.astype(bf16), 1, 0)
    new_error[...] = (merged - approx).astype(bf16)

    stores = [
        pltpu.make_async_copy(src, dst, ls.at[i])
        for i, (src, dst) in enumerate(
            (
                (new_error, new_error_at),
                (new_factor, new_factor_at),
                (new_weight, new_weight_at),
                (new_momentum, new_momentum_at),
            )
        )
    ]
    for store in stores:
        store.start()

    drain(kr, rs.at[14])
    drain(kb.at[pl.ds(0, 4)], rs.at[16])
    base_keys = kb[z].astype(f32) + kr[0].astype(f32) + kr[1].astype(f32)
    for j in range(4):
        base_keys = base_keys + kn[j, 2].astype(f32)
    drain(pp.at[pl.ds(0, nz - 1)], rs.at[9])
    summed = unpack(jnp.sum(pr[...], axis=0)[None], mine // GROUP, rank)[0]
    ortho_padded = jnp.concatenate([ortho, jnp.zeros((LANES - rank, keys), f32)], axis=0)
    turn = dot(summed, ortho_padded, 1, 0, highest)
    own_keys = base_keys - (outer_rate * (1.0 + outer_beta) * scale) * turn
    ga[z] = key_grad(own_keys, cotangent[...].astype(f32), gain[...]).astype(bf16)
    gather_ring(nz, z, ga, ss, rs, 10)
    last = pltpu.make_async_copy(ga, grads_at, ls.at[4])
    last.start()

    drain(pb, ss.at[0])
    drain(ps.at[pl.ds(0, chips - 1)], ss.at[1])
    drain(ps.at[pl.ds(0, chips - 1)], ss.at[2])
    drain(pb, ss.at[3])
    drain(lz.at[pl.ds(0, nz - 1)], ss.at[4])
    drain(ps.at[pl.ds(0, chips - 1)], ss.at[5])
    drain(kb.at[pl.ds(0, 13)], ss.at[13])
    drain(ks, ss.at[14])
    drain(pb, ss.at[7])
    drain(la.at[pl.ds(0, nr - 1)], ss.at[8])
    drain(lq.at[pl.ds(0, nr - 1)], ss.at[15])
    drain(pp.at[pl.ds(0, nz - 1)], ss.at[9])
    for store in stores:
        store.wait()
    last.wait()


def solution(mesh):
    nr, nz = mesh.shape["replica"], mesh.shape["tensor"]
    chips = nr // 2

    def body(tokens, cotangent, drift, error, weight, momentum, factor, gain):
        count, width = tokens.shape
        keys = drift.shape[1]
        rows = weight.shape[0]
        mine = count // nz
        scale = 1.0 / math.sqrt(width * nz)
        state = jax.ShapeDtypeStruct(weight.shape, f32)
        square = jax.ShapeDtypeStruct((keys, width), bf16)
        right = jax.ShapeDtypeStruct(factor.shape, f32)
        in_vmem = pl.BlockSpec(memory_space=pltpu.VMEM)
        in_hbm = pl.BlockSpec(memory_space=pltpu.HBM)
        held = pl.pallas_call(
            functools.partial(kernel, nr, nz, scale),
            out_shape=(
                state,
                state,
                square,
                right,
                jax.ShapeDtypeStruct((nz, mine, keys), bf16),
            ),
            in_specs=[in_hbm] * 8,
            out_specs=(in_hbm,) * 5,
            scratch_shapes=[
                pltpu.VMEM(weight.shape, f32),
                pltpu.VMEM(weight.shape, f32),
                pltpu.VMEM((keys, width), bf16),
                pltpu.VMEM(factor.shape, f32),
                pltpu.VMEM((nz, mine, keys), bf16),
                pltpu.VMEM(tokens.shape, bf16),
                pltpu.VMEM(cotangent.shape, bf16),
                pltpu.VMEM((keys, width), bf16),
                pltpu.VMEM((keys, width), bf16),
                pltpu.VMEM(weight.shape, f32),
                pltpu.VMEM(weight.shape, f32),
                pltpu.VMEM(factor.shape, f32),
                pltpu.VMEM((1, LANES), f32),
                pltpu.VMEM((chips, 2, rows, width), bf16),
                pltpu.VMEM((chips, rows, width), bf16),
                pltpu.VMEM((chips, rows, width), bf16),
                pltpu.VMEM((chips, rows, width), bf16),
                pltpu.VMEM((chips, 2, rows, width), bf16),
                pltpu.VMEM((chips, 2, rows, width), bf16),
                pltpu.VMEM((nr, GROUP // 2, LANES), f32),
                pltpu.VMEM((nr, GROUP // 2, LANES), f32),
                pltpu.VMEM((nz, GROUP // 2, LANES), f32),
                pltpu.VMEM((nr, GROUP // 2, LANES), f32),
                pltpu.VMEM((nr, rows, LANES), f32),
                pltpu.VMEM((nz, mine, keys), bf16),
                pltpu.VMEM((4, 3, mine, keys), bf16),
                pltpu.VMEM((2, mine // 2, keys), bf16),
                pltpu.VMEM((2, mine, keys), bf16),
                pltpu.VMEM((2, mine, keys), bf16),
                pltpu.VMEM((nz, GROUP, LANES), f32),
                pltpu.VMEM((nz, GROUP, LANES), f32),
                pltpu.SemaphoreType.DMA((17,)),
                pltpu.SemaphoreType.DMA((17,)),
                pltpu.SemaphoreType.DMA((8,)),
            ],
            compiler_params=pltpu.CompilerParams(
                collective_id=0, has_side_effects=True, vmem_limit_bytes=GRANT
            ),
            name="outer_inner_step",
        )(
            tokens, cotangent, drift[0], error[0], weight, momentum, factor, gain.reshape(1, -1)
        )
        out = pl.pallas_call(
            functools.partial(finish, scale),
            out_shape=(state, state, square, right, square),
            in_specs=[in_hbm] * 6,
            out_specs=(in_hbm,) * 5,
            scratch_shapes=[
                pltpu.VMEM(weight.shape, f32),
                pltpu.VMEM(weight.shape, f32),
                pltpu.VMEM((keys, width), bf16),
                pltpu.VMEM(factor.shape, f32),
                pltpu.VMEM((count, width), bf16),
                pltpu.VMEM((count, keys), bf16),
                pltpu.VMEM((2, keys // 2, width), bf16),
                pltpu.SemaphoreType.DMA((6,)),
                pltpu.SemaphoreType.DMA((6,)),
            ],
            compiler_params=pltpu.CompilerParams(vmem_limit_bytes=GRANT),
            name="weight_gradient",
        )(*held[:4], tokens, held[4].reshape(count, keys))
        return (out[0], out[1], out[2][None], out[3], out[4][None])

    placed = (
        P("replica", "tensor"),
        P(("replica", "tensor"), None),
        P("replica", None, "tensor"),
        P("replica", None, "tensor"),
        P("replica", "tensor"),
        P("replica", "tensor"),
        P(None, "tensor"),
        P(),
    )
    return jax.shard_map(
        body,
        mesh=mesh,
        in_specs=placed,
        out_specs=(
            P("replica", "tensor"),
            P("replica", "tensor"),
            P("replica", None, "tensor"),
            P(None, "tensor"),
            P("replica", None, "tensor"),
        ),
        check_vma=False,
    )
```
